256 devices in a mesh: dp: 32 (over x, y, core), mp: 8 (over z).
Axes of the slice: x: 4, y: 4, z: 8, core: 2. Of those that a mesh axis runs over, the one named last changes fastest.
Arguments:
- context: bfloat16 [16384, 4096], P('dp', 'mp'), may hold values from -16 to 16
- upstream: bfloat16 [16384, 4096], P('dp'), may hold values from -8 to 8
- out_proj: bfloat16 [4096, 4096], P('mp'), may hold values from -0.09375 to 0.09375
Outputs:
- combined_grad: bfloat16 [4096, 4096], P('mp')
- context_grad: bfloat16 [16384, 4096], P('dp', 'mp')
The draws below stay inside these ranges and needn't reach their ends.
All inputs are finite; a program needn't handle non-finite values.
Results may differ from the reference program's by a relative error of at most 0.001.
The reference program's roundings to bfloat16 on the way count: a program that leaves them out, or rounds other values in their place, can miss the bound.
Values may be sent and summed in bfloat16 or wider, within the bound.
A program may use at most 64 MiB of HBM per device.

```python
import math
import jax
import jax.numpy as jnp
from jax import lax

D = 4096
HD = 4096
TOK_DEV = 512
N_DP = 32
N_MP = 8


def draw_context(key, part):
    key = jax.random.fold_in(key, 11)
    subkeys = jax.random.split(key, 3)
    row_count = TOK_DEV * N_DP
    noise_part = jnp.clip(jax.random.normal(subkeys[0], (row_count, HD), jnp.float32), -6.0, 6.0)
    strength = 0.2
    common = jnp.clip(jax.random.normal(subkeys[1], (HD,), jnp.float32), -4.0, 4.0) * strength
    spread = jnp.exp(jax.random.uniform(subkeys[2], (N_DP, N_MP), jnp.float32, 0.0, math.log(3.0)))
    spread_full = jnp.repeat(jnp.repeat(spread, TOK_DEV, axis=0), HD // N_MP, axis=1)
    ramp_rows = jnp.sqrt(1.0 + 2.0 * jnp.arange(N_DP, dtype=jnp.float32) / max(N_DP - 1, 1))
    ramp_full = jnp.repeat(ramp_rows, TOK_DEV)[:, None]
    return ((noise_part + common[None, :] * spread_full) * ramp_full).astype(jnp.bfloat16)


def draw_upstream(key, part):
    key = jax.random.fold_in(key, 23)
    subkeys = jax.random.split(key, 3)
    row_count = TOK_DEV * N_DP
    noise_part = jnp.clip(jax.random.normal(subkeys[0], (row_count, D), jnp.float32), -6.0, 6.0)
    strength = 0.2
    common = jnp.clip(jax.random.normal(subkeys[1], (D,), jnp.float32), -4.0, 4.0) * strength
    factor = jax.random.uniform(subkeys[2], (N_DP,), jnp.float32, -0.5, 1.5)
    factor_rows = jnp.repeat(factor, TOK_DEV)[:, None]
    return (noise_part + common[None, :] * factor_rows).astype(jnp.bfloat16)


def levels(stream_key, extent, pieces, low, largest):
    factor_of = 1.0
    for axis_at, shards_of in pieces:
        heights = jax.random.uniform(jax.random.fold_in(jax.random.fold_in(stream_key, 6), axis_at), (shards_of,), jnp.float32, low / len(pieces), largest / len(pieces))
        factor_of = factor_of * jnp.repeat(jnp.exp(heights), extent[axis_at] // shards_of).reshape((-1,) + (1,) * (len(extent) - 1 - axis_at))
    return factor_of


def centred(key, shape, scale, most, cuts=(), kind=jnp.bfloat16):
    loudness = levels(key, shape, cuts, -0.22, 0.18) if cuts else 1.0
    entries = jax.random.normal(key, shape, jnp.float32) * scale * loudness
    return jnp.minimum(jnp.maximum(entries, -most), most).astype(kind)


def setup_inputs(seed: int = 0) -> dict:
    splits = jax.random.split(jax.random.key(seed), 4)
    context = draw_context(jax.random.fold_in(splits[3], 71), 0)
    upstream = draw_upstream(jax.random.fold_in(splits[3], 71), 0)
    out_proj = centred(splits[2], (HD, D), D ** -0.5, 0.09375, ((0, 8),))
    return {"context": context, "upstream": upstream, "out_proj": out_proj}


EPSILON = 1e-06

def mix_pair(left, right, crossed, left_norm, right_norm):
    left_wide = left.astype(jnp.float32)
    right_wide = right.astype(jnp.float32)
    mixed = (1.0 - crossed / (2.0 * (left_norm + EPSILON))) * left_wide + (1.0 - crossed / (2.0 * (right_norm + EPSILON))) * right_wide
    return mixed.astype(jnp.bfloat16)

def pair_combine(pair):
    left, right = pair
    left_wide = left.astype(jnp.float32)
    right_wide = right.astype(jnp.float32)
    crossed = jnp.sum(left_wide * right_wide)
    left_norm = jnp.sum(left_wide * left_wide)
    right_norm = jnp.sum(right_wide * right_wide)
    return mix_pair(left, right, crossed, left_norm, right_norm)

def reference(context, upstream, out_proj):
    scaling = 1.0 / math.sqrt(TOK_DEV)
    context_rows = context.reshape(N_DP, TOK_DEV, HD)
    upstream_rows = upstream.reshape(N_DP, TOK_DEV, D)

    def replica_grad(pair):
        ctx_part, up_part = pair
        product = lax.dot_general(ctx_part, up_part, (((0,), (0,)), ((), ())), preferred_element_type=jnp.float32)
        return (product * scaling).astype(jnp.bfloat16)
    vectors = lax.map(replica_grad, (context_rows, upstream_rows))
    while vectors.shape[0] > 1:
        vectors = lax.map(pair_combine, (vectors[0::2], vectors[1::2]))
    context_grad = lax.dot_general(upstream, out_proj, (((1,), (1,)), ((), ())), preferred_element_type=jnp.float32).astype(jnp.bfloat16)
    return (vectors[0], context_grad)
```

```python
import functools
import math

import jax
import jax.numpy as jnp
from jax import lax
from jax.experimental import pallas as pl
from jax.experimental.pallas import tpu as pltpu
from jax.sharding import PartitionSpec as P

EPSILON = 1e-06
MESH = pl.DeviceIdType.MESH
NX, NY, NZ = 4, 4, 8
CHIPS = NX * NY
GROUP = 2 * NZ
TOK = 512
HEADS = 512
HALF = HEADS // 2
ROWS = HALF // CHIPS
WIDTH = 4096
CHUNKS = 8
CW = WIDTH // CHUNKS
PIECES = 4
PW = WIDTH // PIECES
GPIECES = 4
GW = WIDTH // GPIECES


def remote(src, dst, send, recv, device):
    return pltpu.make_async_remote_copy(
        src_ref=src, dst_ref=dst, send_sem=send, recv_sem=recv, device_id=device, device_id_type=MESH
    )


def kernel(
    ctx_hbm, up_hbm, proj_hbm, comb, cgv,
    ctx_own, ctx_sib, up, proj, left_t, sent, own, par, got,
    block, blocks, gram, gblock, gblocks, pblock, pblocks, weights,
    load_sem, up_sem, x_send, x_recv, z_send, z_recv, a_send, a_recv,
    g_send, g_recv, p_send, p_recv, r_send, r_recv, s_send, s_recv,
):
    dp = lax.axis_index("dp")
    z = lax.axis_index("mp")
    core = lax.rem(dp, 2)
    chip = lax.div(dp, 2)
    x = lax.div(chip, NY)
    y = lax.rem(chip, NY)
    place = z * 2 + core
    sibling = (chip * 2 + 1 - core, z)

    def plane_device(t):
        return (t * 2 + core, z)

    def group_device(g):
        return (chip * 2 + lax.rem(g, 2), lax.div(g, 2))

    def plane_peer(k):
        hi, lo = lax.div(k, 4), lax.rem(k, 4)
        dx = jnp.where(core == 0, hi, lo)
        dy = jnp.where(core == 0, lo, hi)
        return lax.rem(x + dx, NX) * NY + lax.rem(y + dy, NY)

    own_cols = pl.ds(pl.multiple_of(core * HALF, HALF), HALF)
    sib_cols = pl.ds(pl.multiple_of((1 - core) * HALF, HALF), HALF)
    load_sib = pltpu.make_async_copy(ctx_hbm.at[:, sib_cols], ctx_sib, load_sem.at[0])
    load_own = pltpu.make_async_copy(ctx_hbm.at[:, own_cols], ctx_own, load_sem.at[1])
    load_proj = pltpu.make_async_copy(proj_hbm, proj, load_sem.at[2])
    load_sib.start()

    def load_up(i):
        cols = pl.ds(pl.multiple_of(i * CW, CW), CW)
        return pltpu.make_async_copy(up_hbm.at[:, cols], up.at[:, cols], up_sem.at[i])

    for i in range(CHUNKS):
        load_up(i).start()
    load_own.start()
    load_proj.start()

    barrier = pltpu.get_barrier_semaphore()

    def greet_group(k, carry):
        pl.semaphore_signal(barrier, inc=1, device_id=group_device(lax.rem(place + k, GROUP)), device_id_type=MESH)
        return carry

    def greet_plane(k, carry):
        pl.semaphore_signal(barrier, inc=1, device_id=plane_device(plane_peer(k)), device_id_type=MESH)
        return carry

    lax.fori_loop(1, GROUP, greet_group, 0)
    lax.fori_loop(1, CHIPS, greet_plane, 0)

    scaling = 1.0 / math.sqrt(TOK)

    def gradient(out):
        def step(i, carry):
            cols = pl.ds(pl.multiple_of(i * CW, CW), CW)
            product = jnp.dot(left_t[...], up[:, cols], preferred_element_type=jnp.float32)
            out[:, cols] = (product * scaling).astype(jnp.bfloat16)
            return carry
        return step

    load_sib.wait()
    left_t[...] = ctx_sib[...].T
    for i in range(CHUNKS):
        load_up(i).wait()
    lax.fori_loop(0, CHUNKS, gradient(sent), 0)
    pl.semaphore_wait(barrier, GROUP - 1 + CHIPS - 1)

    def exchange(i):
        cols = pl.ds(pl.multiple_of(i * CW, CW), CW)
        return remote(sent.at[:, cols], par.at[:, cols], x_send.at[i], x_recv.at[i], sibling)

    def start_exchange(i, carry):
        exchange(i).start()
        return carry

    lax.fori_loop(0, CHUNKS, start_exchange, 0)
    load_own.wait()
    left_t[...] = ctx_own[...].T
    lax.fori_loop(0, CHUNKS, gradient(own), 0)

    zero = jnp.zeros((8, CW), jnp.float32)

    def chunk_sums(i, sums):
        exchange(i).wait_recv()
        cols = pl.ds(pl.multiple_of(i * CW, CW), CW)

        def rows_sums(r, sums):
            crossed, mine, theirs = sums
            rows = pl.ds(pl.multiple_of(r * 16, 16), 16)
            a = own[rows, cols].astype(jnp.float32)
            b = par[rows, cols].astype(jnp.float32)

            def fold(v):
                return v[:8] + v[8:]

            return crossed + fold(a * b), mine + fold(a * a), theirs + fold(b * b)

        return lax.fori_loop(0, HALF // 16, rows_sums, sums, unroll=2)

    crossed, mine, theirs = lax.fori_loop(0, CHUNKS, chunk_sums, (zero, zero, zero))

    def to_row(v):
        v = jnp.sum(v, axis=0, keepdims=True)
        return sum(v[:, j * 128 : (j + 1) * 128] for j in range(CW // 128))

    crossed, mine, theirs = to_row(crossed), to_row(mine), to_row(theirs)
    first = jnp.where(core == 0, mine, theirs)
    second = jnp.where(core == 0, theirs, mine)
    block[...] = jnp.zeros((8, 128), jnp.float32)
    block[0:1, :] = crossed
    block[1:2, :] = first
    block[2:3, :] = second

    def reduce_over(count, me, peer, src, dst, send, recv):
        dst[me] = src[...]

        def copy(k):
            return remote(src, dst.at[me], send.at[k], recv.at[k], peer(k))

        def start(k, carry):
            copy(k).start()
            return carry

        def wait(k, carry):
            copy(k).wait()
            return carry

        lax.fori_loop(1, count, start, 0)
        lax.fori_loop(1, count, wait, 0)
        total = dst[0]
        for i in range(1, count):
            total = total + dst[i]
        return total

    total = reduce_over(
        GROUP, place, lambda k: group_device(lax.rem(place + k, GROUP)), block, blocks, z_send, z_recv
    )
    total = jnp.sum(total, axis=1, keepdims=True)
    crossed, first, second = total[0:1], total[1:2], total[2:3]
    first_by = 1.0 - crossed / (2.0 * (first + EPSILON))
    second_by = 1.0 - crossed / (2.0 * (second + EPSILON))
    own_by = jnp.where(core == 0, first_by, second_by)
    par_by = jnp.where(core == 0, second_by, first_by)

    def mixed(t, p):
        rows = pl.ds(pl.multiple_of(t * ROWS, ROWS), ROWS)
        cols = pl.ds(pl.multiple_of(p * PW, PW), PW)
        a = own[rows, cols].astype(jnp.float32)
        b = par[rows, cols].astype(jnp.float32)
        return (own_by * a + par_by * b).astype(jnp.bfloat16)

    def spread(k, p):
        t = plane_peer(k)
        rows = pl.ds(pl.multiple_of(t * ROWS, ROWS), ROWS)
        to = pl.ds(pl.multiple_of(chip * ROWS, ROWS), ROWS)
        cols = pl.ds(pl.multiple_of(p * PW, PW), PW)
        return remote(own.at[rows, cols], got.at[to, cols], a_send.at[p, k], a_recv.at[p, k], plane_device(t))

    def mix_piece(p, carry):
        def mix_one(k, carry):
            t = plane_peer(k)
            rows = pl.ds(pl.multiple_of(t * ROWS, ROWS), ROWS)
            cols = pl.ds(pl.multiple_of(p * PW, PW), PW)
            own[rows, cols] = mixed(t, p)
            spread(k, p).start()
            return carry

        lax.fori_loop(1, CHIPS, mix_one, 0)
        mine_rows = pl.ds(pl.multiple_of(chip * ROWS, ROWS), ROWS)
        got[mine_rows, pl.ds(pl.multiple_of(p * PW, PW), PW)] = mixed(chip, p)
        return carry

    lax.fori_loop(0, PIECES, mix_piece, 0)

    load_proj.wait()

    def context_rows(i, carry):
        rows = pl.ds(pl.multiple_of(i * 256, 256), 256)
        product = lax.dot_general(
            up[rows, :], proj[...], (((1,), (1,)), ((), ())), preferred_element_type=jnp.float32
        )
        cgv[rows, :] = product.astype(jnp.bfloat16)
        return carry

    lax.fori_loop(0, TOK // 256, context_rows, 0)

    gram[...] = jnp.zeros(gram.shape, jnp.float32)

    def gram_piece(p, carry):
        def wait(k, carry):
            spread(k, p).wait_recv()
            return carry

        lax.fori_loop(1, CHIPS, wait, 0)
        part = got[:, pl.ds(pl.multiple_of(p * PW, PW), PW)]
        gram[...] += lax.dot_general(part, part, (((1,), (1,)), ((), ())), preferred_element_type=jnp.float32)
        return carry

    lax.fori_loop(0, PIECES, gram_piece, 0)
    row_at = lax.broadcasted_iota(jnp.int32, (HALF, HALF), 0)
    col_at = lax.broadcasted_iota(jnp.int32, (HALF, HALF), 1)
    same = lax.rem(row_at, ROWS) == lax.rem(col_at, ROWS)
    by_chip = jnp.sum(jnp.where(same, gram[...], 0.0).reshape(CHIPS, ROWS, HALF), axis=1)
    picks = (
        lax.div(lax.broadcasted_iota(jnp.int32, (HALF, 128), 0), ROWS)
        == lax.broadcasted_iota(jnp.int32, (HALF, 128), 1)
    ).astype(jnp.float32)
    gblock[...] = lax.dot_general(
        by_chip, picks, (((1,), (0,)), ((), ())),
        precision=lax.Precision.HIGHEST, preferred_element_type=jnp.float32,
    )
    pblock[...] = reduce_over(
        GROUP, place, lambda k: group_device(lax.rem(place + k, GROUP)), gblock, gblocks, g_send, g_recv
    )
    products = reduce_over(
        CHIPS, chip, lambda k: plane_device(plane_peer(k)), pblock, pblocks, p_send, p_recv
    )

    at_row = lax.broadcasted_iota(jnp.int32, (CHIPS, 128), 0)
    at_col = lax.broadcasted_iota(jnp.int32, (CHIPS, 128), 1)
    diagonal = at_row == at_col
    for level in range(4):
        step = 1 << level
        row_low = lax.rem(lax.div(at_row, step), 2) == 0
        col_low = lax.rem(lax.div(at_col, step), 2) == 0
        partner = at_col == jnp.where(row_low, at_row + step, at_row - step)
        norm = jnp.sum(jnp.where(diagonal, products, 0.0), axis=1, keepdims=True)
        crossed = jnp.sum(jnp.where(partner, products, 0.0), axis=1, keepdims=True)
        by = 1.0 - crossed / (2.0 * (norm + EPSILON))
        by = jnp.broadcast_to(by, (CHIPS, 128))
        weights[level] = by
        if level < 3:
            by_col = jnp.sum(jnp.where(diagonal, by, 0.0), axis=0, keepdims=True)
            products = by * products * by_col
            swapped = jnp.where(row_low, pltpu.roll(products, CHIPS - step, 0), pltpu.roll(products, step, 0))
            products = products + swapped
            swapped = jnp.where(col_low, pltpu.roll(products, 128 - step, 1), pltpu.roll(products, step, 1))
            products = products + swapped

    a = jnp.where(core == 0, x, y)
    b = jnp.where(core == 0, y, x)

    def chip_at(ra, rb):
        aa = lax.rem(a + ra, 4)
        bb = lax.rem(b + rb, 4)
        return jnp.where(core == 0, aa, bb) * 4 + jnp.where(core == 0, bb, aa)

    def shard(t, c, h):
        rows = pl.ds(pl.multiple_of((c * CHIPS + t) * ROWS, ROWS), ROWS)
        return comb.at[rows, pl.ds(pl.multiple_of(h * GW, GW), GW)]

    my_rows = pl.ds(pl.multiple_of((core * CHIPS + chip) * ROWS, ROWS), ROWS)

    def combine(i, carry):
        cols = pl.ds(pl.multiple_of(i * 128, 128), 128)

        def node(level, start):
            if level < 0:
                return got[start * ROWS : (start + 1) * ROWS, cols].astype(jnp.float32)
            half = 1 << level
            low = node(level - 1, start) * weights[level, start : start + 1, :]
            high = node(level - 1, start + half) * weights[level, start + half : start + half + 1, :]
            result = (low + high).astype(jnp.bfloat16)
            return result if level == 3 else result.astype(jnp.float32)

        comb[my_rows, cols] = node(3, 0)
        return carry

    started = []

    def relay(ra, rb, h, along, k):
        ta, tb = (k, 0) if along == "a" else (0, k)
        da, db = ((ra - k) % 4, rb) if along == "a" else (ra, (rb - k) % 4)
        ref = shard(chip_at(ra, rb), core, h)
        copy = remote(ref, ref, r_send.at[len(started)], r_recv.at[da, db, h], plane_device(chip_at(ta, tb)))
        copy.start()
        started.append(copy)

    siblings = []

    def to_sibling(ra, rb, h):
        ref = shard(chip_at(ra, rb), core, h)
        copy = remote(ref, ref, s_send.at[ra, rb, h], s_recv.at[ra, rb, h], sibling)
        copy.start()
        siblings.append(copy)

    def arrive(ra, rb, h):
        ref = shard(chip_at(ra, rb), core, h)
        remote(ref, ref, r_send.at[0], r_recv.at[ra, rb, h], sibling).wait_recv()

    def along_b(ra, h):
        relay(ra, 0, h, "b", 1)
        relay(ra, 0, h, "b", 3)

    def on_a(ra, h):
        arrive(ra, 0, h)
        if ra == 3 and h < GPIECES // 2:
            relay(3, 0, h, "a", 1)
        if ra == 1 and h >= GPIECES // 2:
            relay(1, 0, h, "a", 3)
        along_b(ra, h)
        to_sibling(ra, 0, h)

    def on_b(ra, rb, h):
        arrive(ra, rb, h)
        if rb == 3 and h < GPIECES // 2:
            relay(ra, 3, h, "b", 1)
        if rb == 1 and h >= GPIECES // 2:
            relay(ra, 1, h, "b", 3)
        to_sibling(ra, rb, h)

    for h in range(GPIECES):
        lax.fori_loop(h * (GW // 128), (h + 1) * (GW // 128), combine, 0)
        relay(0, 0, h, "a", 1)
        relay(0, 0, h, "a", 3)
        along_b(0, h)
        to_sibling(0, 0, h)
    for h in range(GPIECES):
        on_a(3, h)
        on_a(1, h)
    for h in range(GPIECES):
        on_b(0, 3, h)
        on_b(0, 1, h)
    for h in range(GPIECES):
        on_a(2, h)
    for ra in (3, 1, 2):
        for h in range(GPIECES):
            on_b(ra, 3, h)
            on_b(ra, 1, h)
    for ra in (0, 3, 1, 2):
        for h in range(GPIECES):
            arrive(ra, 2, h)
            to_sibling(ra, 2, h)

    for copy in started:
        copy.wait_send()
    for copy in siblings:
        copy.wait_send()
    for ra in range(4):
        for rb in range(4):
            for h in range(GPIECES):
                ref = shard(chip_at(rb, ra), 1 - core, h)
                remote(ref, ref, s_send.at[0, 0, 0], s_recv.at[ra, rb, h], sibling).wait_recv()

    def end_exchange(i, carry):
        exchange(i).wait_send()
        return carry

    lax.fori_loop(0, CHUNKS, end_exchange, 0)

    def end_piece(p, carry):
        def wait(k, carry):
            spread(k, p).wait_send()
            return carry

        return lax.fori_loop(1, CHIPS, wait, carry)

    lax.fori_loop(0, PIECES, end_piece, 0)


def shards(context, upstream, out_proj):
    bf16, f32 = jnp.bfloat16, jnp.float32
    vmem, dma = pltpu.VMEM, pltpu.SemaphoreType.DMA
    return pl.pallas_call(
        kernel,
        out_shape=(OUT_COMB, OUT_CG),
        in_specs=[pl.BlockSpec(memory_space=pltpu.HBM)] * 3,
        out_specs=(pl.BlockSpec(memory_space=pltpu.VMEM), pl.BlockSpec(memory_space=pltpu.VMEM)),
        scratch_shapes=[
            vmem((TOK, HALF), bf16),
            vmem((TOK, HALF), bf16),
            vmem((TOK, WIDTH), bf16),
            vmem((HEADS, WIDTH), bf16),
            vmem((HALF, TOK), bf16),
            vmem((HALF, WIDTH), bf16),
            vmem((HALF, WIDTH), bf16),
            vmem((HALF, WIDTH), bf16),
            vmem((HALF, WIDTH), bf16),
            vmem((8, 128), f32),
            vmem((GROUP, 8, 128), f32),
            vmem((HALF, HALF), f32),
            vmem((CHIPS, 128), f32),
            vmem((GROUP, CHIPS, 128), f32),
            vmem((CHIPS, 128), f32),
            vmem((CHIPS, CHIPS, 128), f32),
            vmem((4, CHIPS, 128), f32),
            dma((3,)),
            dma((CHUNKS,)),
            dma((CHUNKS,)),
            dma((CHUNKS,)),
            dma((GROUP,)),
            dma((GROUP,)),
            dma((PIECES, CHIPS)),
            dma((PIECES, CHIPS)),
            dma((GROUP,)),
            dma((GROUP,)),
            dma((CHIPS,)),
            dma((CHIPS,)),
            dma((15 * GPIECES,)),
            dma((4, 4, GPIECES)),
            dma((4, 4, GPIECES)),
            dma((4, 4, GPIECES)),
        ],
        compiler_params=pltpu.CompilerParams(
            collective_id=0, has_side_effects=True, vmem_limit_bytes=40 << 20
        ),
        cost_estimate=pl.CostEstimate(flops=8 << 30, bytes_accessed=14 << 20, transcendentals=0),
    )(context, upstream, out_proj)


OUT_COMB = jax.ShapeDtypeStruct((HEADS, WIDTH), jnp.bfloat16)
OUT_CG = jax.ShapeDtypeStruct((TOK, HEADS), jnp.bfloat16)


def solution(mesh):
    in_specs = (P("dp", "mp"), P("dp", None), P("mp", None))
    out_specs = (P("mp", None), P("dp", "mp"))
    return jax.shard_map(shards, mesh=mesh, in_specs=in_specs, out_specs=out_specs, check_vma=False)
```

```python
import functools
import math

import jax
import jax.numpy as jnp
from jax import lax
from jax.experimental import pallas as pl
from jax.experimental.pallas import tpu as pltpu
from jax.sharding import PartitionSpec as P

EPSILON = 1e-06
MESH = pl.DeviceIdType.MESH
NX, NY, NZ = 4, 4, 8
CHIPS = NX * NY
GROUP = 2 * NZ
TOK = 512
HEADS = 512
HALF = HEADS // 2
ROWS = HALF // CHIPS
WIDTH = 4096
CHUNKS = 8
CW = WIDTH // CHUNKS
PIECES = 4
PW = WIDTH // PIECES
GPIECES = 4
GW = WIDTH // GPIECES


def receive_semaphores():
    index, group = {}, {}
    for ra in range(4):
        for rb in range(4):
            for h in range(GPIECES):
                if rb == 2:
                    key = (ra, rb)
                elif (rb == 3 and h >= GPIECES // 2) or (rb == 1 and h < GPIECES // 2):
                    key = (ra, rb, "rest")
                else:
                    key = (ra, rb, h)
                if (ra, rb) != (0, 0):
                    index[ra, rb, h] = group.setdefault(key, len(group))
    return index, len(group)


RECV, N_RECV = receive_semaphores()


def remote(src, dst, send, recv, device):
    return pltpu.make_async_remote_copy(
        src_ref=src, dst_ref=dst, send_sem=send, recv_sem=recv, device_id=device, device_id_type=MESH
    )


def kernel(
    ctx_hbm, up_hbm, proj_hbm, comb, cgv,
    ctx_own, ctx_sib, up, proj, left_t, sent, own, par, got,
    block, blocks, gram, gblock, gblocks, pblock, pblocks, weights,
    load_sem, up_sem, x_send, x_recv, z_send, z_recv, a_send, a_recv,
    g_send, g_recv, p_send, p_recv, r_send, r_recv, s_send, s_recv,
):
    dp = lax.axis_index("dp")
    z = lax.axis_index("mp")
    core = lax.rem(dp, 2)
    chip = lax.div(dp, 2)
    x = lax.div(chip, NY)
    y = lax.rem(chip, NY)
    place = z * 2 + core
    sibling = (chip * 2 + 1 - core, z)

    def plane_device(t):
        return (t * 2 + core, z)

    def group_device(g):
        return (chip * 2 + lax.rem(g, 2), lax.div(g, 2))

    def plane_peer(k):
        hi, lo = lax.div(k, 4), lax.rem(k, 4)
        dx = jnp.where(core == 0, hi, lo)
        dy = jnp.where(core == 0, lo, hi)
        return lax.rem(x + dx, NX) * NY + lax.rem(y + dy, NY)

    own_cols = pl.ds(pl.multiple_of(core * HALF, HALF), HALF)
    sib_cols = pl.ds(pl.multiple_of((1 - core) * HALF, HALF), HALF)
    load_sib = pltpu.make_async_copy(ctx_hbm.at[:, sib_cols], ctx_sib, load_sem.at[0])
    load_own = pltpu.make_async_copy(ctx_hbm.at[:, own_cols], ctx_own, load_sem.at[1])
    load_proj = pltpu.make_async_copy(proj_hbm, proj, load_sem.at[2])
    load_sib.start()

    def load_up(i):
        cols = pl.ds(pl.multiple_of(i * CW, CW), CW)
        return pltpu.make_async_copy(up_hbm.at[:, cols], up.at[:, cols], up_sem)

    for i in range(CHUNKS):
        load_up(i).start()
    load_own.start()
    load_proj.start()

    barrier = pltpu.get_barrier_semaphore()

    def greet_group(k, carry):
        pl.semaphore_signal(barrier, inc=1, device_id=group_device(lax.rem(place + k, GROUP)), device_id_type=MESH)
        return carry

    def greet_plane(k, carry):
        pl.semaphore_signal(barrier, inc=1, device_id=plane_device(plane_peer(k)), device_id_type=MESH)
        return carry

    lax.fori_loop(1, GROUP, greet_group, 0)
    lax.fori_loop(1, CHIPS, greet_plane, 0)

    scaling = 1.0 / math.sqrt(TOK)

    def gradient(out):
        def step(i, carry):
            cols = pl.ds(pl.multiple_of(i * CW, CW), CW)
            product = jnp.dot(left_t[...], up[:, cols], preferred_element_type=jnp.float32)
            out[:, cols] = (product * scaling).astype(jnp.bfloat16)
            return carry
        return step

    load_sib.wait()
    left_t[...] = ctx_sib[...].T
    pltpu.make_async_copy(up_hbm, up, up_sem).wait()
    lax.fori_loop(0, CHUNKS, gradient(sent), 0)
    pl.semaphore_wait(barrier, GROUP - 1 + CHIPS - 1)

    def exchange(i):
        cols = pl.ds(pl.multiple_of(i * CW, CW), CW)
        return remote(sent.at[:, cols], par.at[:, cols], x_send, x_recv.at[i], sibling)

    def start_exchange(i, carry):
        exchange(i).start()
        return carry

    lax.fori_loop(0, CHUNKS, start_exchange, 0)
    load_own.wait()
    left_t[...] = ctx_own[...].T
    lax.fori_loop(0, CHUNKS, gradient(own), 0)

    zero = jnp.zeros((8, CW), jnp.float32)

    def chunk_sums(i, sums):
        exchange(i).wait_recv()
        cols = pl.ds(pl.multiple_of(i * CW, CW), CW)

        def rows_sums(r, sums):
            crossed, mine, theirs = sums
            rows = pl.ds(pl.multiple_of(r * 16, 16), 16)
            a = own[rows, cols].astype(jnp.float32)
            b = par[rows, cols].astype(jnp.float32)

            def fold(v):
                return v[:8] + v[8:]

            return crossed + fold(a * b), mine + fold(a * a), theirs + fold(b * b)

        return lax.fori_loop(0, HALF // 16, rows_sums, sums, unroll=2)

    crossed, mine, theirs = lax.fori_loop(0, CHUNKS, chunk_sums, (zero, zero, zero))

    def to_row(v):
        v = jnp.sum(v, axis=0, keepdims=True)
        return sum(v[:, j * 128 : (j + 1) * 128] for j in range(CW // 128))

    crossed, mine, theirs = to_row(crossed), to_row(mine), to_row(theirs)
    first = jnp.where(core == 0, mine, theirs)
    second = jnp.where(core == 0, theirs, mine)
    block[...] = jnp.zeros((8, 128), jnp.float32)
    block[0:1, :] = crossed
    block[1:2, :] = first
    block[2:3, :] = second

    def reduce_over(count, me, peer, src, dst, send, recv):
        dst[me] = src[...]

        def start(k, carry):
            remote(src, dst.at[me], send, recv, peer(k)).start()
            return carry

        lax.fori_loop(1, count, start, 0)
        others = dst.at[pl.ds(0, count - 1)]
        remote(others, others, send, recv, sibling).wait()
        total = dst[0]
        for i in range(1, count):
            total = total + dst[i]
        return total

    total = reduce_over(
        GROUP, place, lambda k: group_device(lax.rem(place + k, GROUP)), block, blocks, z_send, z_recv
    )
    total = jnp.sum(total, axis=1, keepdims=True)
    crossed, first, second = total[0:1], total[1:2], total[2:3]
    first_by = 1.0 - crossed / (2.0 * (first + EPSILON))
    second_by = 1.0 - crossed / (2.0 * (second + EPSILON))
    own_by = jnp.where(core == 0, first_by, second_by)
    par_by = jnp.where(core == 0, second_by, first_by)

    def mixed(t, p):
        rows = pl.ds(pl.multiple_of(t * ROWS, ROWS), ROWS)
        cols = pl.ds(pl.multiple_of(p * PW, PW), PW)
        a = own[rows, cols].astype(jnp.float32)
        b = par[rows, cols].astype(jnp.float32)
        return (own_by * a + par_by * b).astype(jnp.bfloat16)

    def spread(k, p):
        t = plane_peer(k)
        rows = pl.ds(pl.multiple_of(t * ROWS, ROWS), ROWS)
        to = pl.ds(pl.multiple_of(chip * ROWS, ROWS), ROWS)
        cols = pl.ds(pl.multiple_of(p * PW, PW), PW)
        return remote(own.at[rows, cols], got.at[to, cols], a_send, a_recv.at[p], plane_device(t))

    def mix_piece(p, carry):
        def mix_one(k, carry):
            t = plane_peer(k)
            rows = pl.ds(pl.multiple_of(t * ROWS, ROWS), ROWS)
            cols = pl.ds(pl.multiple_of(p * PW, PW), PW)
            own[rows, cols] = mixed(t, p)
            spread(k, p).start()
            return carry

        lax.fori_loop(1, CHIPS, mix_one, 0)
        mine_rows = pl.ds(pl.multiple_of(chip * ROWS, ROWS), ROWS)
        got[mine_rows, pl.ds(pl.multiple_of(p * PW, PW), PW)] = mixed(chip, p)
        return carry

    lax.fori_loop(0, PIECES, mix_piece, 0)

    load_proj.wait()

    def context_rows(i, carry):
        rows = pl.ds(pl.multiple_of(i * 256, 256), 256)
        product = lax.dot_general(
            up[rows, :], proj[...], (((1,), (1,)), ((), ())), preferred_element_type=jnp.float32
        )
        cgv[rows, :] = product.astype(jnp.bfloat16)
        return carry

    lax.fori_loop(0, TOK // 256, context_rows, 0)

    gram[...] = jnp.zeros(gram.shape, jnp.float32)

    def gram_piece(p, carry):
        others = got.at[pl.ds(0, HALF - ROWS), pl.ds(pl.multiple_of(p * PW, PW), PW)]
        remote(others, others, a_send, a_recv.at[p], sibling).wait_recv()
        part = got[:, pl.ds(pl.multiple_of(p * PW, PW), PW)]
        gram[...] += lax.dot_general(part, part, (((1,), (1,)), ((), ())), preferred_element_type=jnp.float32)
        return carry

    lax.fori_loop(0, PIECES, gram_piece, 0)
    row_at = lax.broadcasted_iota(jnp.int32, (HALF, HALF), 0)
    col_at = lax.broadcasted_iota(jnp.int32, (HALF, HALF), 1)
    same = lax.rem(row_at, ROWS) == lax.rem(col_at, ROWS)
    by_chip = jnp.sum(jnp.where(same, gram[...], 0.0).reshape(CHIPS, ROWS, HALF), axis=1)
    picks = (
        lax.div(lax.broadcasted_iota(jnp.int32, (HALF, 128), 0), ROWS)
        == lax.broadcasted_iota(jnp.int32, (HALF, 128), 1)
    ).astype(jnp.float32)
    products = lax.dot_general(
        by_chip, picks, (((1,), (0,)), ((), ())),
        precision=lax.Precision.HIGHEST, preferred_element_type=jnp.float32,
    )
    gblock[...] = products[:8] + pltpu.roll(products[8:], CHIPS, 1)
    pblock[...] = reduce_over(
        GROUP, place, lambda k: group_device(lax.rem(place + k, GROUP)), gblock, gblocks, g_send, g_recv
    )
    packed = reduce_over(
        CHIPS, chip, lambda k: plane_device(plane_peer(k)), pblock, pblocks, p_send, p_recv
    )

    at_row = lax.broadcasted_iota(jnp.int32, (CHIPS, 128), 0)
    at_col = lax.broadcasted_iota(jnp.int32, (CHIPS, 128), 1)
    products = jnp.concatenate([packed, pltpu.roll(packed, 128 - CHIPS, 1)], axis=0)
    products = jnp.where(at_col < CHIPS, products, 0.0)
    diagonal = at_row == at_col
    for level in range(4):
        step = 1 << level
        row_low = lax.rem(lax.div(at_row, step), 2) == 0
        col_low = lax.rem(lax.div(at_col, step), 2) == 0
        partner = at_col == jnp.where(row_low, at_row + step, at_row - step)
        norm = jnp.sum(jnp.where(diagonal, products, 0.0), axis=1, keepdims=True)
        crossed = jnp.sum(jnp.where(partner, products, 0.0), axis=1, keepdims=True)
        by = 1.0 - crossed / (2.0 * (norm + EPSILON))
        by = jnp.broadcast_to(by, (CHIPS, 128))
        weights[level] = by
        if level < 3:
            by_col = jnp.sum(jnp.where(diagonal, by, 0.0), axis=0, keepdims=True)
            products = by * products * by_col
            swapped = jnp.where(row_low, pltpu.roll(products, CHIPS - step, 0), pltpu.roll(products, step, 0))
            products = products + swapped
            swapped = jnp.where(col_low, pltpu.roll(products, 128 - step, 1), pltpu.roll(products, step, 1))
            products = products + swapped

    a = jnp.where(core == 0, x, y)
    b = jnp.where(core == 0, y, x)

    def chip_at(ra, rb):
        aa = lax.rem(a + ra, 4)
        bb = lax.rem(b + rb, 4)
        return jnp.where(core == 0, aa, bb) * 4 + jnp.where(core == 0, bb, aa)

    def shard(t, c, h, count=1):
        rows = pl.ds(pl.multiple_of((c * CHIPS + t) * ROWS, ROWS), ROWS)
        return comb.at[rows, pl.ds(h * GW, count * GW)]

    my_rows = pl.ds(pl.multiple_of((core * CHIPS + chip) * ROWS, ROWS), ROWS)

    def combine(i, carry):
        cols = pl.ds(pl.multiple_of(i * 128, 128), 128)

        def node(level, start):
            if level < 0:
                return got[start * ROWS : (start + 1) * ROWS, cols].astype(jnp.float32)
            half = 1 << level
            low = node(level - 1, start) * weights[level, start : start + 1, :]
            high = node(level - 1, start + half) * weights[level, start + half : start + half + 1, :]
            result = (low + high).astype(jnp.bfloat16)
            return result if level == 3 else result.astype(jnp.float32)

        comb[my_rows, cols] = node(3, 0)
        return carry

    def relay(ra, rb, h, along, k):
        ta, tb = (k, 0) if along == "a" else (0, k)
        da, db = ((ra - k) % 4, rb) if along == "a" else (ra, (rb - k) % 4)
        ref = shard(chip_at(ra, rb), core, h)
        remote(ref, ref, r_send, r_recv.at[RECV[da, db, h]], plane_device(chip_at(ta, tb))).start()

    def to_sibling(ra, rb, h, count=1):
        ref = shard(chip_at(ra, rb), core, h, count)
        remote(ref, ref, s_send, s_recv, sibling).start()

    def arrive(ra, rb, h, count=1):
        ref = shard(chip_at(ra, rb), core, h, count)
        remote(ref, ref, r_send, r_recv.at[RECV[ra, rb, h]], sibling).wait_recv()

    def along_b(ra, h):
        relay(ra, 0, h, "b", 1)
        relay(ra, 0, h, "b", 3)

    def on_a(ra, h):
        arrive(ra, 0, h)
        if ra == 3 and h < GPIECES // 2:
            relay(3, 0, h, "a", 1)
        if ra == 1 and h >= GPIECES // 2:
            relay(1, 0, h, "a", 3)
        along_b(ra, h)
        to_sibling(ra, 0, h)

    HB = GPIECES // 2

    def relayed(ra, h):
        arrive(ra, 3, h)
        relay(ra, 3, h, "b", 1)
        arrive(ra, 1, h + HB)
        relay(ra, 1, h + HB, "b", 3)

    def ended(ra):
        to_sibling(ra, 3, 0, HB)
        to_sibling(ra, 1, HB, HB)
        arrive(ra, 3, HB, HB)
        to_sibling(ra, 3, HB, HB)
        arrive(ra, 1, 0, HB)
        to_sibling(ra, 1, 0, HB)

    for h in range(GPIECES):
        lax.fori_loop(h * (GW // 128), (h + 1) * (GW // 128), combine, 0)
        relay(0, 0, h, "a", 1)
        relay(0, 0, h, "a", 3)
        along_b(0, h)
    to_sibling(0, 0, 0, GPIECES)
    for h in range(GPIECES):
        on_a(3, h)
        on_a(1, h)
    for h in range(HB):
        relayed(0, h)
    for h in range(GPIECES):
        on_a(2, h)
    for ra in (3, 1, 2):
        for h in range(HB):
            relayed(ra, h)
    for ra in (0, 3, 1, 2):
        ended(ra)
    for ra in (0, 3, 1, 2):
        arrive(ra, 2, 0, GPIECES)
        to_sibling(ra, 2, 0, GPIECES)

    mine = comb.at[pl.ds(0, HALF - ROWS)]
    remote(mine, mine, r_send, r_recv.at[0], sibling).wait_send()
    theirs = comb.at[pl.ds(0, HALF)]
    remote(theirs, theirs, s_send, s_recv, sibling).wait()
    remote(sent, par, x_send, x_recv.at[0], sibling).wait_send()

    others = got.at[pl.ds(0, HALF - ROWS)]
    remote(others, others, a_send, a_recv.at[0], sibling).wait_send()


OUT_PARTS = 4


def store(comb, cgv, comb_hbm, cg_hbm, sems):
    copies = [pltpu.make_async_copy(cgv, cg_hbm, sems.at[OUT_PARTS])]
    for i in range(OUT_PARTS):
        rows = pl.ds(i * (HEADS // OUT_PARTS), HEADS // OUT_PARTS)
        copies.append(pltpu.make_async_copy(comb.at[rows], comb_hbm.at[rows], sems.at[i]))
    for copy in copies:
        copy.start()
    for copy in copies:
        copy.wait()


def shards(context, upstream, out_proj):
    context, upstream, out_proj = (
        pltpu.with_memory_space_constraint(v, pltpu.HBM) for v in (context, upstream, out_proj)
    )
    bf16, f32 = jnp.bfloat16, jnp.float32
    vmem, dma = pltpu.VMEM, pltpu.SemaphoreType.DMA
    results = pl.pallas_call(
        kernel,
        out_shape=(OUT_COMB, OUT_CG),
        in_specs=[pl.BlockSpec(memory_space=pltpu.HBM)] * 3,
        out_specs=(pl.BlockSpec(memory_space=pltpu.VMEM), pl.BlockSpec(memory_space=pltpu.VMEM)),
        scratch_shapes=[
            vmem((TOK, HALF), bf16),
            vmem((TOK, HALF), bf16),
            vmem((TOK, WIDTH), bf16),
            vmem((HEADS, WIDTH), bf16),
            vmem((HALF, TOK), bf16),
            vmem((HALF, WIDTH), bf16),
            vmem((HALF, WIDTH), bf16),
            vmem((HALF, WIDTH), bf16),
            vmem((HALF, WIDTH), bf16),
            vmem((8, 128), f32),
            vmem((GROUP, 8, 128), f32),
            vmem((HALF, HALF), f32),
            vmem((8, 128), f32),
            vmem((GROUP, 8, 128), f32),
            vmem((8, 128), f32),
            vmem((CHIPS, 8, 128), f32),
            vmem((4, CHIPS, 128), f32),
            dma((3,)),
            dma,
            dma,
            dma((CHUNKS,)),
            dma,
            dma,
            dma,
            dma((PIECES,)),
            dma,
            dma,
            dma,
            dma,
            dma,
            dma((N_RECV,)),
            dma,
            dma,
        ],
        compiler_params=pltpu.CompilerParams(
            collective_id=0, has_side_effects=True, vmem_limit_bytes=40 << 20
        ),
        cost_estimate=pl.CostEstimate(flops=8 << 30, bytes_accessed=14 << 20, transcendentals=0),
    )(context, upstream, out_proj)
    return pl.pallas_call(
        store,
        out_shape=(OUT_COMB, OUT_CG),
        in_specs=[pl.BlockSpec(memory_space=pl.ANY)] * 2,
        out_specs=[pl.BlockSpec(memory_space=pltpu.HBM)] * 2,
        compiler_params=pltpu.CompilerParams(vmem_limit_bytes=1 << 20),
        scratch_shapes=[pltpu.SemaphoreType.DMA((OUT_PARTS + 1,))],
    )(*results)


OUT_COMB = jax.ShapeDtypeStruct((HEADS, WIDTH), jnp.bfloat16)
OUT_CG = jax.ShapeDtypeStruct((TOK, HEADS), jnp.bfloat16)


def solution(mesh):
    in_specs = (P("dp", "mp"), P("dp", None), P("mp", None))
    out_specs = (P("mp", None), P("dp", "mp"))
    return jax.shard_map(shards, mesh=mesh, in_specs=in_specs, out_specs=out_specs, check_vma=False)
```

```python
import functools
import math

import jax
import jax.numpy as jnp
from jax import lax
from jax.experimental import pallas as pl
from jax.experimental.pallas import tpu as pltpu
from jax.sharding import PartitionSpec as P

EPSILON = 1e-06
MESH = pl.DeviceIdType.MESH
NX, NY, NZ = 4, 4, 8
CHIPS = NX * NY
GROUP = 2 * NZ
TOK = 512
HEADS = 512
HALF = HEADS // 2
ROWS = HALF // CHIPS
WIDTH = 4096
CHUNKS = 8
CW = WIDTH // CHUNKS
PIECES = 16
PW = WIDTH // PIECES
EARLY = 1
FIRSTP = 2
RAWP = 3
FIRST = FIRSTP * PW
RAW = RAWP * PW
GPIECES = 4
GW = WIDTH // GPIECES


def receive_semaphores():
    index, group = {}, {}
    for ra in range(4):
        for rb in range(4):
            for h in range(GPIECES):
                if rb == 2:
                    key = (ra, rb)
                elif (rb == 3 and h >= GPIECES // 2) or (rb == 1 and h < GPIECES // 2):
                    key = (ra, rb, "rest")
                else:
                    key = (ra, rb, h)
                if (ra, rb) != (0, 0):
                    index[ra, rb, h] = group.setdefault(key, len(group))
    return index, len(group)


RECV, N_RECV = receive_semaphores()


def remote(src, dst, send, recv, device):
    return pltpu.make_async_remote_copy(
        src_ref=src, dst_ref=dst, send_sem=send, recv_sem=recv, device_id=device, device_id_type=MESH
    )


def kernel(
    ctx_hbm, up_hbm, proj_hbm, comb, cgv,
    ctx_own, ctx_sib, up, proj, left_t, sent, own, par, got,
    raw, factor, factors, block, blocks, gram, gblock, gblocks, pblock, pblocks, weights,
    load_sem, up_sem, x_send, x_recv, z_send, z_recv, a_send, a_recv,
    w_send, w_recv, f_send, f_recv, g_send, g_recv, p_send, p_recv, r_send, r_recv, s_send, s_recv,
):
    dp = lax.axis_index("dp")
    z = lax.axis_index("mp")
    core = lax.rem(dp, 2)
    chip = lax.div(dp, 2)
    x = lax.div(chip, NY)
    y = lax.rem(chip, NY)
    place = z * 2 + core
    sibling = (chip * 2 + 1 - core, z)

    def plane_device(t):
        return (t * 2 + core, z)

    def group_device(g):
        return (chip * 2 + lax.rem(g, 2), lax.div(g, 2))

    def plane_peer(k):
        hi, lo = lax.div(k, 4), lax.rem(k, 4)
        dx = jnp.where(core == 0, hi, lo)
        dy = jnp.where(core == 0, lo, hi)
        return lax.rem(x + dx, NX) * NY + lax.rem(y + dy, NY)

    own_cols = pl.ds(pl.multiple_of(core * HALF, HALF), HALF)
    sib_cols = pl.ds(pl.multiple_of((1 - core) * HALF, HALF), HALF)
    load_sib = pltpu.make_async_copy(ctx_hbm.at[:, sib_cols], ctx_sib, load_sem.at[0])
    load_own = pltpu.make_async_copy(ctx_hbm.at[:, own_cols], ctx_own, load_sem.at[1])
    load_proj = pltpu.make_async_copy(proj_hbm, proj, load_sem.at[2])
    load_sib.start()

    def load_up(i):
        cols = pl.ds(pl.multiple_of(i * CW, CW), CW)
        return pltpu.make_async_copy(up_hbm.at[:, cols], up.at[:, cols], up_sem)

    for i in range(CHUNKS):
        load_up(i).start()
    load_own.start()
    load_proj.start()

    barrier = pltpu.get_barrier_semaphore()

    def greet_group(k, carry):
        pl.semaphore_signal(barrier, inc=1, device_id=group_device(lax.rem(place + k, GROUP)), device_id_type=MESH)
        return carry

    def greet_plane(k, carry):
        pl.semaphore_signal(barrier, inc=1, device_id=plane_device(plane_peer(k)), device_id_type=MESH)
        return carry

    lax.fori_loop(1, GROUP, greet_group, 0)
    lax.fori_loop(1, CHIPS, greet_plane, 0)

    scaling = 1.0 / math.sqrt(TOK)

    def gradient(out):
        def step(i, carry):
            cols = pl.ds(pl.multiple_of(i * CW, CW), CW)
            product = jnp.dot(left_t[...], up[:, cols], preferred_element_type=jnp.float32)
            out[:, cols] = (product * scaling).astype(jnp.bfloat16)
            return carry
        return step

    load_sib.wait()
    left_t[...] = ctx_sib[...].T
    pltpu.make_async_copy(up_hbm, up, up_sem).wait()
    lax.fori_loop(0, CHUNKS, gradient(sent), 0)
    load_own.wait()
    left_t[...] = ctx_own[...].T
    lax.fori_loop(0, EARLY, gradient(own), 0)
    pl.semaphore_wait(barrier, GROUP - 1 + CHIPS - 1)

    def exchange(i):
        cols = pl.ds(pl.multiple_of(i * CW, CW), CW)
        return remote(sent.at[:, cols], par.at[:, cols], x_send, x_recv.at[i], sibling)

    def start_exchange(i, carry):
        exchange(i).start()
        return carry

    lax.fori_loop(0, CHUNKS, start_exchange, 0)

    def spread_raw(values, replica, begin, end):
        def start(k, carry):
            t = plane_peer(k)
            rows = pl.ds(pl.multiple_of(t * ROWS, ROWS), ROWS)
            to = pl.ds(pl.multiple_of(chip * ROWS, ROWS), ROWS)
            remote(
                values.at[rows, pl.ds(begin, end - begin)],
                raw.at[replica, to, pl.ds(begin, end - begin)],
                w_send, w_recv, plane_device(t),
            ).start()
            return carry

        if end > begin:
            lax.fori_loop(1, CHIPS, start, 0)

    lax.fori_loop(EARLY, max(FIRST // CW, EARLY), gradient(own), 0)
    spread_raw(own, core, 0, FIRST)
    lax.fori_loop(max(FIRST // CW, EARLY), CHUNKS, gradient(own), 0)

    zero = jnp.zeros((8, CW), jnp.float32)

    def chunk_sums(i, sums):
        exchange(i).wait_recv()
        cols = pl.ds(pl.multiple_of(i * CW, CW), CW)

        def rows_sums(r, sums):
            crossed, mine, theirs = sums
            rows = pl.ds(pl.multiple_of(r * 16, 16), 16)
            a = own[rows, cols].astype(jnp.float32)
            b = par[rows, cols].astype(jnp.float32)

            def fold(v):
                return v[:8] + v[8:]

            return crossed + fold(a * b), mine + fold(a * a), theirs + fold(b * b)

        return lax.fori_loop(0, HALF // 16, rows_sums, sums, unroll=2)

    sums = lax.fori_loop(0, FIRST // CW, chunk_sums, (zero, zero, zero))
    spread_raw(par, 1 - core, 0, FIRST)
    crossed, mine, theirs = lax.fori_loop(FIRST // CW, CHUNKS, chunk_sums, sums)

    lane = lax.broadcasted_iota(jnp.int32, (1, 128), 1)

    def total_of(v):
        return jnp.sum(jnp.sum(v, axis=0, keepdims=True), axis=1, keepdims=True)

    crossed, mine, theirs = total_of(crossed), total_of(mine), total_of(theirs)
    first = jnp.where(core == 0, mine, theirs)
    second = jnp.where(core == 0, theirs, mine)
    block[...] = jnp.where(lane == 0, crossed, jnp.where(lane == 1, first, jnp.where(lane == 2, second, 0.0)))

    def reduce_over(count, me, peer, src, dst, send, recv, meanwhile=lambda: None):
        dst[me] = src[...]

        def start(k, carry):
            remote(src, dst.at[me], send, recv, peer(k)).start()
            return carry

        lax.fori_loop(1, count, start, 0)
        meanwhile()
        others = dst.at[pl.ds(0, count - 1)]
        remote(others, others, send, recv, sibling).wait()
        total = dst[0]
        for i in range(1, count):
            total = total + dst[i]
        return total

    def more_raw():
        spread_raw(own, core, FIRST, RAW)
        spread_raw(par, 1 - core, FIRST, RAW)

    total = reduce_over(
        GROUP, place, lambda k: group_device(lax.rem(place + k, GROUP)), block, blocks, z_send, z_recv, more_raw
    )
    crossed, first, second = (
        jnp.sum(jnp.where(lane == i, total, 0.0), axis=1, keepdims=True) for i in range(3)
    )
    first_by = 1.0 - crossed / (2.0 * (first + EPSILON))
    second_by = 1.0 - crossed / (2.0 * (second + EPSILON))
    own_by = jnp.where(core == 0, first_by, second_by)
    par_by = jnp.where(core == 0, second_by, first_by)

    if RAWP:
        factor[0:1, :] = jnp.broadcast_to(first_by, (1, 128))
        factor[1:2, :] = jnp.broadcast_to(second_by, (1, 128))

        def send_factor(k, carry):
            remote(factor, factors.at[chip], f_send, f_recv, plane_device(plane_peer(k))).start()
            return carry

        lax.fori_loop(1, CHIPS, send_factor, 0)

    def mixed(t, p):
        rows = pl.ds(pl.multiple_of(t * ROWS, ROWS), ROWS)
        cols = pl.ds(pl.multiple_of(p * PW, PW), PW)
        a = own[rows, cols].astype(jnp.float32)
        b = par[rows, cols].astype(jnp.float32)
        return (own_by * a + par_by * b).astype(jnp.bfloat16)

    def spread(k, p):
        t = plane_peer(k)
        rows = pl.ds(pl.multiple_of(t * ROWS, ROWS), ROWS)
        to = pl.ds(pl.multiple_of(chip * ROWS, ROWS), ROWS)
        cols = pl.ds(pl.multiple_of(p * PW, PW), PW)
        return remote(own.at[rows, cols], got.at[to, cols], a_send, a_recv.at[p], plane_device(t))

    def mix_piece(p, carry):
        def mix_one(k, carry):
            t = plane_peer(k)
            rows = pl.ds(pl.multiple_of(t * ROWS, ROWS), ROWS)
            cols = pl.ds(pl.multiple_of(p * PW, PW), PW)
            own[rows, cols] = mixed(t, p)
            spread(k, p).start()
            return carry

        lax.fori_loop(1, CHIPS, mix_one, 0)
        mine_rows = pl.ds(pl.multiple_of(chip * ROWS, ROWS), ROWS)
        got[mine_rows, pl.ds(pl.multiple_of(p * PW, PW), PW)] = mixed(chip, p)
        return carry

    lax.fori_loop(RAWP, PIECES, mix_piece, 0)

    if RAWP:
        others = raw.at[:, pl.ds(0, HALF - ROWS)]
        remote(others, others, w_send, w_recv, sibling).wait()
        others = factors.at[pl.ds(0, CHIPS - 1)]
        remote(others, others, f_send, f_recv, sibling).wait()

        def mix_raw(k, carry):
            t = plane_peer(k)
            rows = pl.ds(pl.multiple_of(t * ROWS, ROWS), ROWS)
            by = factors[t]
            left = raw[0, rows, :].astype(jnp.float32)
            right = raw[1, rows, :].astype(jnp.float32)
            got[rows, pl.ds(0, RAW)] = (by[0:1, 0:1] * left + by[1:2, 0:1] * right).astype(jnp.bfloat16)
            return carry

        lax.fori_loop(1, CHIPS, mix_raw, 0)

        def mix_own(p, carry):
            mine_rows = pl.ds(pl.multiple_of(chip * ROWS, ROWS), ROWS)
            got[mine_rows, pl.ds(pl.multiple_of(p * PW, PW), PW)] = mixed(chip, p)
            return carry

        lax.fori_loop(0, RAWP, mix_own, 0)

    load_proj.wait()

    def context_rows(i, carry):
        rows = pl.ds(pl.multiple_of(i * 256, 256), 256)
        product = lax.dot_general(
            up[rows, :], proj[...], (((1,), (1,)), ((), ())), preferred_element_type=jnp.float32
        )
        cgv[rows, :] = product.astype(jnp.bfloat16)
        return carry

    lax.fori_loop(0, TOK // 256, context_rows, 0)

    gram[...] = jnp.zeros(gram.shape, jnp.float32)

    def gram_piece(p, carry):
        @pl.when(p >= RAWP)
        def _():
            others = got.at[pl.ds(0, HALF - ROWS), pl.ds(pl.multiple_of(p * PW, PW), PW)]
            remote(others, others, a_send, a_recv.at[p], sibling).wait_recv()

        part = got[:, pl.ds(pl.multiple_of(p * PW, PW), PW)]
        gram[...] += lax.dot_general(part, part, (((1,), (1,)), ((), ())), preferred_element_type=jnp.float32)
        return carry

    lax.fori_loop(0, PIECES, gram_piece, 0)
    row_at = lax.broadcasted_iota(jnp.int32, (HALF, HALF), 0)
    col_at = lax.broadcasted_iota(jnp.int32, (HALF, HALF), 1)
    same = lax.rem(row_at, ROWS) == lax.rem(col_at, ROWS)
    by_chip = jnp.sum(jnp.where(same, gram[...], 0.0).reshape(CHIPS, ROWS, HALF), axis=1)
    picks = (
        lax.div(lax.broadcasted_iota(jnp.int32, (HALF, 128), 0), ROWS)
        == lax.rem(lax.broadcasted_iota(jnp.int32, (HALF, 128), 1), CHIPS)
    ).astype(jnp.float32)
    products = lax.dot_general(
        by_chip, picks, (((1,), (0,)), ((), ())),
        precision=lax.Precision.HIGHEST, preferred_element_type=jnp.float32,
    )
    at_row = lax.broadcasted_iota(jnp.int32, (CHIPS, 128), 0)
    at_col = lax.broadcasted_iota(jnp.int32, (CHIPS, 128), 1)
    in_group = lax.div(at_col, CHIPS) == lax.rem(at_row, 8)
    products = jnp.where(in_group, products, 0.0)
    gblock[0:1, :] = jnp.sum(products[:8], axis=0, keepdims=True)
    gblock[1:2, :] = jnp.sum(products[8:], axis=0, keepdims=True)
    pblock[...] = reduce_over(
        GROUP, place, lambda k: group_device(lax.rem(place + k, GROUP)), gblock, gblocks, g_send, g_recv
    )
    packed = reduce_over(
        CHIPS, chip, lambda k: plane_device(plane_peer(k)), pblock, pblocks, p_send, p_recv
    )

    products = jnp.concatenate(
        [jnp.broadcast_to(packed[0:1], (8, 128)), jnp.broadcast_to(packed[1:2], (8, 128))], axis=0
    )
    products = jnp.where(in_group, products, 0.0)
    for shift in (16, 32, 64):
        products = products + pltpu.roll(products, shift, 1)
    products = jnp.where(at_col < CHIPS, products, 0.0)
    diagonal = at_row == at_col
    for level in range(4):
        step = 1 << level
        row_low = lax.rem(lax.div(at_row, step), 2) == 0
        col_low = lax.rem(lax.div(at_col, step), 2) == 0
        partner = at_col == jnp.where(row_low, at_row + step, at_row - step)
        norm = jnp.sum(jnp.where(diagonal, products, 0.0), axis=1, keepdims=True)
        crossed = jnp.sum(jnp.where(partner, products, 0.0), axis=1, keepdims=True)
        by = 1.0 - crossed / (2.0 * (norm + EPSILON))
        by = jnp.broadcast_to(by, (CHIPS, 128))
        weights[level] = by
        if level < 3:
            by_col = jnp.sum(jnp.where(diagonal, by, 0.0), axis=0, keepdims=True)
            products = by * products * by_col
            swapped = jnp.where(row_low, pltpu.roll(products, CHIPS - step, 0), pltpu.roll(products, step, 0))
            products = products + swapped
            swapped = jnp.where(col_low, pltpu.roll(products, 128 - step, 1), pltpu.roll(products, step, 1))
            products = products + swapped

    a = jnp.where(core == 0, x, y)
    b = jnp.where(core == 0, y, x)

    def chip_at(ra, rb):
        aa = lax.rem(a + ra, 4)
        bb = lax.rem(b + rb, 4)
        return jnp.where(core == 0, aa, bb) * 4 + jnp.where(core == 0, bb, aa)

    def shard(t, c, h, count=1):
        rows = pl.ds(pl.multiple_of((c * CHIPS + t) * ROWS, ROWS), ROWS)
        return comb.at[rows, pl.ds(h * GW, count * GW)]

    my_rows = pl.ds(pl.multiple_of((core * CHIPS + chip) * ROWS, ROWS), ROWS)

    def combine(i, carry):
        cols = pl.ds(pl.multiple_of(i * 128, 128), 128)

        def node(level, start):
            if level < 0:
                return got[start * ROWS : (start + 1) * ROWS, cols].astype(jnp.float32)
            half = 1 << level
            low = node(level - 1, start) * weights[level, start : start + 1, :]
            high = node(level - 1, start + half) * weights[level, start + half : start + half + 1, :]
            result = (low + high).astype(jnp.bfloat16)
            return result if level == 3 else result.astype(jnp.float32)

        comb[my_rows, cols] = node(3, 0)
        return carry

    def relay(ra, rb, h, along, k):
        ta, tb = (k, 0) if along == "a" else (0, k)
        da, db = ((ra - k) % 4, rb) if along == "a" else (ra, (rb - k) % 4)
        ref = shard(chip_at(ra, rb), core, h)
        remote(ref, ref, r_send, r_recv.at[RECV[da, db, h]], plane_device(chip_at(ta, tb))).start()

    def to_sibling(ra, rb, h, count=1):
        ref = shard(chip_at(ra, rb), core, h, count)
        remote(ref, ref, s_send, s_recv, sibling).start()

    def arrive(ra, rb, h, count=1):
        ref = shard(chip_at(ra, rb), core, h, count)
        remote(ref, ref, r_send, r_recv.at[RECV[ra, rb, h]], sibling).wait_recv()

    def along_b(ra, h):
        relay(ra, 0, h, "b", 1)
        relay(ra, 0, h, "b", 3)

    def on_a(ra, h):
        arrive(ra, 0, h)
        if ra == 3 and h < GPIECES // 2:
            relay(3, 0, h, "a", 1)
        if ra == 1 and h >= GPIECES // 2:
            relay(1, 0, h, "a", 3)
        along_b(ra, h)
        to_sibling(ra, 0, h)

    HB = GPIECES // 2

    def relayed(ra, h):
        arrive(ra, 3, h)
        relay(ra, 3, h, "b", 1)
        arrive(ra, 1, h + HB)
        relay(ra, 1, h + HB, "b", 3)

    def ended(ra):
        to_sibling(ra, 3, 0, HB)
        to_sibling(ra, 1, HB, HB)
        arrive(ra, 3, HB, HB)
        to_sibling(ra, 3, HB, HB)
        arrive(ra, 1, 0, HB)
        to_sibling(ra, 1, 0, HB)

    for h in range(GPIECES):
        lax.fori_loop(h * (GW // 128), (h + 1) * (GW // 128), combine, 0)
        relay(0, 0, h, "a", 1)
        relay(0, 0, h, "a", 3)
        along_b(0, h)
    to_sibling(0, 0, 0, GPIECES)
    for h in range(GPIECES):
        on_a(3, h)
        on_a(1, h)
    for h in range(HB):
        relayed(0, h)
    for h in range(GPIECES):
        on_a(2, h)
    for ra in (3, 1, 2):
        for h in range(HB):
            relayed(ra, h)
    for ra in (0, 3, 1, 2):
        ended(ra)
    for ra in (0, 3, 1, 2):
        arrive(ra, 2, 0, GPIECES)
        to_sibling(ra, 2, 0, GPIECES)

    mine = comb.at[pl.ds(0, HALF - ROWS)]
    remote(mine, mine, r_send, r_recv.at[0], sibling).wait_send()
    theirs = comb.at[pl.ds(0, HALF)]
    remote(theirs, theirs, s_send, s_recv, sibling).wait()
    remote(sent, par, x_send, x_recv.at[0], sibling).wait_send()

    others = got.at[pl.ds(0, HALF - ROWS), pl.ds(RAW, WIDTH - RAW)]
    remote(others, others, a_send, a_recv.at[0], sibling).wait_send()


OUT_PARTS = 4


def store(comb, cgv, comb_hbm, cg_hbm, sems):
    copies = [pltpu.make_async_copy(cgv, cg_hbm, sems.at[OUT_PARTS])]
    for i in range(OUT_PARTS):
        rows = pl.ds(i * (HEADS // OUT_PARTS), HEADS // OUT_PARTS)
        copies.append(pltpu.make_async_copy(comb.at[rows], comb_hbm.at[rows], sems.at[i]))
    for copy in copies:
        copy.start()
    for copy in copies:
        copy.wait()


def shards(context, upstream, out_proj):
    context, upstream, out_proj = (
        pltpu.with_memory_space_constraint(v, pltpu.HBM) for v in (context, upstream, out_proj)
    )
    bf16, f32 = jnp.bfloat16, jnp.float32
    vmem, dma = pltpu.VMEM, pltpu.SemaphoreType.DMA
    results = pl.pallas_call(
        kernel,
        out_shape=(OUT_COMB, OUT_CG),
        in_specs=[pl.BlockSpec(memory_space=pltpu.HBM)] * 3,
        out_specs=(pl.BlockSpec(memory_space=pltpu.VMEM), pl.BlockSpec(memory_space=pltpu.VMEM)),
        scratch_shapes=[
            vmem((TOK, HALF), bf16),
            vmem((TOK, HALF), bf16),
            vmem((TOK, WIDTH), bf16),
            vmem((HEADS, WIDTH), bf16),
            vmem((HALF, TOK), bf16),
            vmem((HALF, WIDTH), bf16),
            vmem((HALF, WIDTH), bf16),
            vmem((HALF, WIDTH), bf16),
            vmem((HALF, WIDTH), bf16),
            vmem((2, HALF, max(RAW, 128)), bf16),
            vmem((8, 128), f32),
            vmem((CHIPS, 8, 128), f32),
            vmem((1, 128), f32),
            vmem((GROUP, 1, 128), f32),
            vmem((HALF, HALF), f32),
            vmem((2, 128), f32),
            vmem((GROUP, 2, 128), f32),
            vmem((2, 128), f32),
            vmem((CHIPS, 2, 128), f32),
            vmem((4, CHIPS, 128), f32),
            dma((3,)),
            dma,
            dma,
            dma((CHUNKS,)),
            dma,
            dma,
            dma,
            dma((PIECES,)),
            dma,
            dma,
            dma,
            dma,
            dma,
            dma,
            dma,
            dma,
            dma,
            dma((N_RECV,)),
            dma,
            dma,
        ],
        compiler_params=pltpu.CompilerParams(
            collective_id=0, has_side_effects=True, vmem_limit_bytes=40 << 20
        ),
        cost_estimate=pl.CostEstimate(flops=8 << 30, bytes_accessed=14 << 20, transcendentals=0),
    )(context, upstream, out_proj)
    return pl.pallas_call(
        store,
        out_shape=(OUT_COMB, OUT_CG),
        in_specs=[pl.BlockSpec(memory_space=pl.ANY)] * 2,
        out_specs=[pl.BlockSpec(memory_space=pltpu.HBM)] * 2,
        compiler_params=pltpu.CompilerParams(vmem_limit_bytes=1 << 20),
        scratch_shapes=[pltpu.SemaphoreType.DMA((OUT_PARTS + 1,))],
    )(*results)


OUT_COMB = jax.ShapeDtypeStruct((HEADS, WIDTH), jnp.bfloat16)
OUT_CG = jax.ShapeDtypeStruct((TOK, HEADS), jnp.bfloat16)


def solution(mesh):
    in_specs = (P("dp", "mp"), P("dp", None), P("mp", None))
    out_specs = (P("mp", None), P("dp", "mp"))
    return jax.shard_map(shards, mesh=mesh, in_specs=in_specs, out_specs=out_specs, check_vma=False)
```

```python
import functools
import math

import jax
import jax.numpy as jnp
from jax import lax
from jax.experimental import pallas as pl
from jax.experimental.pallas import tpu as pltpu
from jax.sharding import PartitionSpec as P

EPSILON = 1e-06
MESH = pl.DeviceIdType.MESH
NX, NY, NZ = 4, 4, 8
CHIPS = NX * NY
GROUP = 2 * NZ
TOK = 512
HEADS = 512
HALF = HEADS // 2
ROWS = HALF // CHIPS
WIDTH = 4096
CHUNKS = 8
CW = WIDTH // CHUNKS
PIECES = 16
PW = WIDTH // PIECES
EARLY = 1
FIRSTP = 2
RAWP = 3
FIRST = FIRSTP * PW
RAW = RAWP * PW
GPIECES = 4
GW = WIDTH // GPIECES


def receive_semaphores():
    index, group = {}, {}
    for ra in range(4):
        for rb in range(4):
            for h in range(GPIECES):
                if rb == 2:
                    key = (ra, rb)
                elif (rb == 3 and h >= GPIECES // 2) or (rb == 1 and h < GPIECES // 2):
                    key = (ra, rb, "rest")
                else:
                    key = (ra, rb, h)
                if (ra, rb) != (0, 0):
                    index[ra, rb, h] = group.setdefault(key, len(group))
    return index, len(group)


RECV, N_RECV = receive_semaphores()


def remote(src, dst, send, recv, device):
    return pltpu.make_async_remote_copy(
        src_ref=src, dst_ref=dst, send_sem=send, recv_sem=recv, device_id=device, device_id_type=MESH
    )


def kernel(
    ctx_hbm, up_hbm, proj_hbm, comb, cgv,
    ctx_own, ctx_sib, up, proj, left_t, sent, own, par, got,
    raw, factor, factors, block, blocks, gram, gblock, gblocks, pblock, pblocks, weights,
    load_sem, up_sem, x_send, x_recv, z_send, z_recv, a_send, a_recv,
    w_send, w_recv, f_send, f_recv, g_send, g_recv, p_send, p_recv, r_send, r_recv, s_send, s_recv,
):
    dp = lax.axis_index("dp")
    z = lax.axis_index("mp")
    core = lax.rem(dp, 2)
    chip = lax.div(dp, 2)
    x = lax.div(chip, NY)
    y = lax.rem(chip, NY)
    place = z * 2 + core
    sibling = (chip * 2 + 1 - core, z)

    def plane_device(t):
        return (t * 2 + core, z)

    def group_device(g):
        return (chip * 2 + lax.rem(g, 2), lax.div(g, 2))

    def plane_peer(k):
        hi, lo = lax.div(k, 4), lax.rem(k, 4)
        dx = jnp.where(core == 0, hi, lo)
        dy = jnp.where(core == 0, lo, hi)
        return lax.rem(x + dx, NX) * NY + lax.rem(y + dy, NY)

    own_cols = pl.ds(pl.multiple_of(core * HALF, HALF), HALF)
    sib_cols = pl.ds(pl.multiple_of((1 - core) * HALF, HALF), HALF)
    load_sib = pltpu.make_async_copy(ctx_hbm.at[:, sib_cols], ctx_sib, load_sem.at[0])
    load_own = pltpu.make_async_copy(ctx_hbm.at[:, own_cols], ctx_own, load_sem.at[1])
    load_proj = pltpu.make_async_copy(proj_hbm, proj, load_sem.at[2])
    load_sib.start()

    def load_up(i):
        cols = pl.ds(pl.multiple_of(i * CW, CW), CW)
        return pltpu.make_async_copy(up_hbm.at[:, cols], up.at[:, cols], up_sem)

    for i in range(CHUNKS):
        load_up(i).start()
    load_own.start()
    load_proj.start()

    barrier = pltpu.get_barrier_semaphore()

    def greet_group(k, carry):
        pl.semaphore_signal(barrier, inc=1, device_id=group_device(lax.rem(place + k, GROUP)), device_id_type=MESH)
        return carry

    def greet_plane(k, carry):
        pl.semaphore_signal(barrier, inc=1, device_id=plane_device(plane_peer(k)), device_id_type=MESH)
        return carry

    lax.fori_loop(1, GROUP, greet_group, 0)
    lax.fori_loop(1, CHIPS, greet_plane, 0)

    scaling = 1.0 / math.sqrt(TOK)

    def gradient(out):
        def step(i, carry):
            cols = pl.ds(pl.multiple_of(i * CW, CW), CW)
            product = jnp.dot(left_t[...], up[:, cols], preferred_element_type=jnp.float32)
            out[:, cols] = (product * scaling).astype(jnp.bfloat16)
            return carry
        return step

    load_sib.wait()
    left_t[...] = ctx_sib[...].T
    pltpu.make_async_copy(up_hbm, up, up_sem).wait()
    lax.fori_loop(0, CHUNKS, gradient(sent), 0)
    load_own.wait()
    left_t[...] = ctx_own[...].T
    lax.fori_loop(0, EARLY, gradient(own), 0)
    pl.semaphore_wait(barrier, GROUP - 1 + CHIPS - 1)

    def exchange(i):
        cols = pl.ds(pl.multiple_of(i * CW, CW), CW)
        return remote(sent.at[:, cols], par.at[:, cols], x_send, x_recv.at[i], sibling)

    def start_exchange(i, carry):
        exchange(i).start()
        return carry

    lax.fori_loop(0, CHUNKS, start_exchange, 0)

    def spread_raw(values, replica, begin, end):
        def start(k, carry):
            t = plane_peer(k)
            rows = pl.ds(pl.multiple_of(t * ROWS, ROWS), ROWS)
            to = pl.ds(pl.multiple_of(chip * ROWS, ROWS), ROWS)
            remote(
                values.at[rows, pl.ds(begin, end - begin)],
                raw.at[replica, to, pl.ds(begin, end - begin)],
                w_send, w_recv, plane_device(t),
            ).start()
            return carry

        if end > begin:
            lax.fori_loop(1, CHIPS, start, 0)

    lax.fori_loop(EARLY, max(FIRST // CW, EARLY), gradient(own), 0)
    spread_raw(own, core, 0, FIRST)
    lax.fori_loop(max(FIRST // CW, EARLY), CHUNKS, gradient(own), 0)

    zero = jnp.zeros((8, CW), jnp.float32)

    def chunk_sums(i, sums):
        exchange(i).wait_recv()
        cols = pl.ds(pl.multiple_of(i * CW, CW), CW)

        def rows_sums(r, sums):
            crossed, mine, theirs = sums
            rows = pl.ds(pl.multiple_of(r * 16, 16), 16)
            a = own[rows, cols].astype(jnp.float32)
            b = par[rows, cols].astype(jnp.float32)

            def fold(v):
                return v[:8] + v[8:]

            return crossed + fold(a * b), mine + fold(a * a), theirs + fold(b * b)

        return lax.fori_loop(0, HALF // 16, rows_sums, sums, unroll=8)

    sums = lax.fori_loop(0, FIRST // CW, chunk_sums, (zero, zero, zero))
    spread_raw(par, 1 - core, 0, FIRST)
    crossed, mine, theirs = lax.fori_loop(FIRST // CW, CHUNKS, chunk_sums, sums)

    lane = lax.broadcasted_iota(jnp.int32, (1, 128), 1)

    def total_of(v):
        return jnp.sum(jnp.sum(v, axis=0, keepdims=True), axis=1, keepdims=True)

    crossed, mine, theirs = total_of(crossed), total_of(mine), total_of(theirs)
    first = jnp.where(core == 0, mine, theirs)
    second = jnp.where(core == 0, theirs, mine)
    block[...] = jnp.where(lane == 0, crossed, jnp.where(lane == 1, first, jnp.where(lane == 2, second, 0.0)))

    def reduce_over(count, me, peer, src, dst, send, recv, meanwhile=lambda: None):
        dst[me] = src[...]

        def start(k, carry):
            remote(src, dst.at[me], send, recv, peer(k)).start()
            return carry

        lax.fori_loop(1, count, start, 0)
        meanwhile()
        others = dst.at[pl.ds(0, count - 1)]
        remote(others, others, send, recv, sibling).wait()
        total = dst[0]
        for i in range(1, count):
            total = total + dst[i]
        return total

    def more_raw():
        spread_raw(own, core, FIRST, RAW)
        spread_raw(par, 1 - core, FIRST, RAW)

    total = reduce_over(
        GROUP, place, lambda k: group_device(lax.rem(place + k, GROUP)), block, blocks, z_send, z_recv, more_raw
    )
    crossed, first, second = (
        jnp.sum(jnp.where(lane == i, total, 0.0), axis=1, keepdims=True) for i in range(3)
    )
    first_by = 1.0 - crossed / (2.0 * (first + EPSILON))
    second_by = 1.0 - crossed / (2.0 * (second + EPSILON))
    own_by = jnp.where(core == 0, first_by, second_by)
    par_by = jnp.where(core == 0, second_by, first_by)

    if RAWP:
        factor[0:1, :] = jnp.broadcast_to(first_by, (1, 128))
        factor[1:2, :] = jnp.broadcast_to(second_by, (1, 128))

        def send_factor(k, carry):
            remote(factor, factors.at[chip], f_send, f_recv, plane_device(plane_peer(k))).start()
            return carry

        lax.fori_loop(1, CHIPS, send_factor, 0)

    def mixed(t, p):
        rows = pl.ds(pl.multiple_of(t * ROWS, ROWS), ROWS)
        cols = pl.ds(pl.multiple_of(p * PW, PW), PW)
        a = own[rows, cols].astype(jnp.float32)
        b = par[rows, cols].astype(jnp.float32)
        return (own_by * a + par_by * b).astype(jnp.bfloat16)

    def spread(k, p):
        t = plane_peer(k)
        rows = pl.ds(pl.multiple_of(t * ROWS, ROWS), ROWS)
        to = pl.ds(pl.multiple_of(chip * ROWS, ROWS), ROWS)
        cols = pl.ds(pl.multiple_of(p * PW, PW), PW)
        return remote(own.at[rows, cols], got.at[to, cols], a_send, a_recv.at[p], plane_device(t))

    def mix_piece(p, carry):
        def mix_one(k, carry):
            t = plane_peer(k)
            rows = pl.ds(pl.multiple_of(t * ROWS, ROWS), ROWS)
            cols = pl.ds(pl.multiple_of(p * PW, PW), PW)
            own[rows, cols] = mixed(t, p)
            spread(k, p).start()
            return carry

        lax.fori_loop(1, CHIPS, mix_one, 0)
        mine_rows = pl.ds(pl.multiple_of(chip * ROWS, ROWS), ROWS)
        got[mine_rows, pl.ds(pl.multiple_of(p * PW, PW), PW)] = mixed(chip, p)
        return carry

    lax.fori_loop(RAWP, PIECES, mix_piece, 0)

    if RAWP:
        others = raw.at[:, pl.ds(0, HALF - ROWS)]
        remote(others, others, w_send, w_recv, sibling).wait()
        others = factors.at[pl.ds(0, CHIPS - 1)]
        remote(others, others, f_send, f_recv, sibling).wait()

        def mix_raw(k, carry):
            t = plane_peer(k)
            rows = pl.ds(pl.multiple_of(t * ROWS, ROWS), ROWS)
            by = factors[t]
            left = raw[0, rows, :].astype(jnp.float32)
            right = raw[1, rows, :].astype(jnp.float32)
            got[rows, pl.ds(0, RAW)] = (by[0:1, 0:1] * left + by[1:2, 0:1] * right).astype(jnp.bfloat16)
            return carry

        lax.fori_loop(1, CHIPS, mix_raw, 0)

        def mix_own(p, carry):
            mine_rows = pl.ds(pl.multiple_of(chip * ROWS, ROWS), ROWS)
            got[mine_rows, pl.ds(pl.multiple_of(p * PW, PW), PW)] = mixed(chip, p)
            return carry

        lax.fori_loop(0, RAWP, mix_own, 0)

    load_proj.wait()

    def context_rows(i, carry):
        rows = pl.ds(pl.multiple_of(i * 256, 256), 256)
        product = lax.dot_general(
            up[rows, :], proj[...], (((1,), (1,)), ((), ())), preferred_element_type=jnp.float32
        )
        cgv[rows, :] = product.astype(jnp.bfloat16)
        return carry

    lax.fori_loop(0, TOK // 256, context_rows, 0)

    gram[...] = jnp.zeros(gram.shape, jnp.float32)

    def gram_piece(p, carry):
        @pl.when(p >= RAWP)
        def _():
            others = got.at[pl.ds(0, HALF - ROWS), pl.ds(pl.multiple_of(p * PW, PW), PW)]
            remote(others, others, a_send, a_recv.at[p], sibling).wait_recv()

        part = got[:, pl.ds(pl.multiple_of(p * PW, PW), PW)]
        gram[...] += lax.dot_general(part, part, (((1,), (1,)), ((), ())), preferred_element_type=jnp.float32)
        return carry

    lax.fori_loop(0, PIECES, gram_piece, 0)
    row_at = lax.broadcasted_iota(jnp.int32, (HALF, HALF), 0)
    col_at = lax.broadcasted_iota(jnp.int32, (HALF, HALF), 1)
    same = lax.rem(row_at, ROWS) == lax.rem(col_at, ROWS)
    by_chip = jnp.sum(jnp.where(same, gram[...], 0.0).reshape(CHIPS, ROWS, HALF), axis=1)
    picks = (
        lax.div(lax.broadcasted_iota(jnp.int32, (HALF, 128), 0), ROWS)
        == lax.rem(lax.broadcasted_iota(jnp.int32, (HALF, 128), 1), CHIPS)
    ).astype(jnp.float32)
    products = lax.dot_general(
        by_chip, picks, (((1,), (0,)), ((), ())),
        precision=lax.Precision.HIGHEST, preferred_element_type=jnp.float32,
    )
    at_row = lax.broadcasted_iota(jnp.int32, (CHIPS, 128), 0)
    at_col = lax.broadcasted_iota(jnp.int32, (CHIPS, 128), 1)
    in_group = lax.div(at_col, CHIPS) == lax.rem(at_row, 8)
    products = jnp.where(in_group, products, 0.0)
    gblock[0:1, :] = jnp.sum(products[:8], axis=0, keepdims=True)
    gblock[1:2, :] = jnp.sum(products[8:], axis=0, keepdims=True)
    pblock[...] = reduce_over(
        GROUP, place, lambda k: group_device(lax.rem(place + k, GROUP)), gblock, gblocks, g_send, g_recv
    )
    packed = reduce_over(
        CHIPS, chip, lambda k: plane_device(plane_peer(k)), pblock, pblocks, p_send, p_recv
    )

    products = jnp.concatenate(
        [jnp.broadcast_to(packed[0:1], (8, 128)), jnp.broadcast_to(packed[1:2], (8, 128))], axis=0
    )
    products = jnp.where(in_group, products, 0.0)
    for shift in (16, 32, 64):
        products = products + pltpu.roll(products, shift, 1)
    products = jnp.where(at_col < CHIPS, products, 0.0)
    diagonal = at_row == at_col
    for level in range(4):
        step = 1 << level
        row_low = lax.rem(lax.div(at_row, step), 2) == 0
        col_low = lax.rem(lax.div(at_col, step), 2) == 0
        partner = at_col == jnp.where(row_low, at_row + step, at_row - step)
        norm = jnp.sum(jnp.where(diagonal, products, 0.0), axis=1, keepdims=True)
        crossed = jnp.sum(jnp.where(partner, products, 0.0), axis=1, keepdims=True)
        by = 1.0 - crossed / (2.0 * (norm + EPSILON))
        by = jnp.broadcast_to(by, (CHIPS, 128))
        weights[level] = by
        if level < 3:
            by_col = jnp.sum(jnp.where(diagonal, by, 0.0), axis=0, keepdims=True)
            products = by * products * by_col
            swapped = jnp.where(row_low, pltpu.roll(products, CHIPS - step, 0), pltpu.roll(products, step, 0))
            products = products + swapped
            swapped = jnp.where(col_low, pltpu.roll(products, 128 - step, 1), pltpu.roll(products, step, 1))
            products = products + swapped

    a = jnp.where(core == 0, x, y)
    b = jnp.where(core == 0, y, x)

    def chip_at(ra, rb):
        aa = lax.rem(a + ra, 4)
        bb = lax.rem(b + rb, 4)
        return jnp.where(core == 0, aa, bb) * 4 + jnp.where(core == 0, bb, aa)

    def shard(t, c, h, count=1):
        rows = pl.ds(pl.multiple_of((c * CHIPS + t) * ROWS, ROWS), ROWS)
        return comb.at[rows, pl.ds(h * GW, count * GW)]

    my_rows = pl.ds(pl.multiple_of((core * CHIPS + chip) * ROWS, ROWS), ROWS)

    def combine(i, carry):
        cols = pl.ds(pl.multiple_of(i * 128, 128), 128)

        def node(level, start):
            if level < 0:
                return got[start * ROWS : (start + 1) * ROWS, cols].astype(jnp.float32)
            half = 1 << level
            low = node(level - 1, start) * weights[level, start : start + 1, :]
            high = node(level - 1, start + half) * weights[level, start + half : start + half + 1, :]
            result = (low + high).astype(jnp.bfloat16)
            return result if level == 3 else result.astype(jnp.float32)

        comb[my_rows, cols] = node(3, 0)
        return carry

    def relay(ra, rb, h, along, k):
        ta, tb = (k, 0) if along == "a" else (0, k)
        da, db = ((ra - k) % 4, rb) if along == "a" else (ra, (rb - k) % 4)
        ref = shard(chip_at(ra, rb), core, h)
        remote(ref, ref, r_send, r_recv.at[RECV[da, db, h]], plane_device(chip_at(ta, tb))).start()

    def to_sibling(ra, rb, h, count=1):
        ref = shard(chip_at(ra, rb), core, h, count)
        remote(ref, ref, s_send, s_recv, sibling).start()

    def arrive(ra, rb, h, count=1):
        ref = shard(chip_at(ra, rb), core, h, count)
        remote(ref, ref, r_send, r_recv.at[RECV[ra, rb, h]], sibling).wait_recv()

    def along_b(ra, h):
        relay(ra, 0, h, "b", 1)
        relay(ra, 0, h, "b", 3)

    def on_a(ra, h):
        arrive(ra, 0, h)
        if ra == 3 and h < GPIECES // 2:
            relay(3, 0, h, "a", 1)
        if ra == 1 and h >= GPIECES // 2:
            relay(1, 0, h, "a", 3)
        along_b(ra, h)
        to_sibling(ra, 0, h)

    HB = GPIECES // 2

    def relayed(ra, h):
        arrive(ra, 3, h)
        relay(ra, 3, h, "b", 1)
        arrive(ra, 1, h + HB)
        relay(ra, 1, h + HB, "b", 3)

    def ended(ra):
        to_sibling(ra, 3, 0, HB)
        to_sibling(ra, 1, HB, HB)
        arrive(ra, 3, HB, HB)
        to_sibling(ra, 3, HB, HB)
        arrive(ra, 1, 0, HB)
        to_sibling(ra, 1, 0, HB)

    for h in range(GPIECES):
        lax.fori_loop(h * (GW // 128), (h + 1) * (GW // 128), combine, 0)
        relay(0, 0, h, "a", 1)
        relay(0, 0, h, "a", 3)
        along_b(0, h)
    to_sibling(0, 0, 0, GPIECES)
    for h in range(GPIECES):
        on_a(3, h)
        on_a(1, h)
    for h in range(HB):
        relayed(0, h)
    for h in range(GPIECES):
        on_a(2, h)
    for ra in (3, 1, 2):
        for h in range(HB):
            relayed(ra, h)
    for ra in (0, 3, 1, 2):
        ended(ra)
    for ra in (0, 3, 1, 2):
        arrive(ra, 2, 0, GPIECES)
        to_sibling(ra, 2, 0, GPIECES)

    mine = comb.at[pl.ds(0, HALF - ROWS)]
    remote(mine, mine, r_send, r_recv.at[0], sibling).wait_send()
    theirs = comb.at[pl.ds(0, HALF)]
    remote(theirs, theirs, s_send, s_recv, sibling).wait()
    remote(sent, par, x_send, x_recv.at[0], sibling).wait_send()

    others = got.at[pl.ds(0, HALF - ROWS), pl.ds(RAW, WIDTH - RAW)]
    remote(others, others, a_send, a_recv.at[0], sibling).wait_send()


OUT_PARTS = 4


def store(comb, cgv, comb_hbm, cg_hbm, sems):
    copies = [pltpu.make_async_copy(cgv, cg_hbm, sems.at[OUT_PARTS])]
    for i in range(OUT_PARTS):
        rows = pl.ds(i * (HEADS // OUT_PARTS), HEADS // OUT_PARTS)
        copies.append(pltpu.make_async_copy(comb.at[rows], comb_hbm.at[rows], sems.at[i]))
    for copy in copies:
        copy.start()
    for copy in copies:
        copy.wait()


def shards(context, upstream, out_proj):
    context, upstream, out_proj = (
        pltpu.with_memory_space_constraint(v, pltpu.HBM) for v in (context, upstream, out_proj)
    )
    bf16, f32 = jnp.bfloat16, jnp.float32
    vmem, dma = pltpu.VMEM, pltpu.SemaphoreType.DMA
    results = pl.pallas_call(
        kernel,
        out_shape=(OUT_COMB, OUT_CG),
        in_specs=[pl.BlockSpec(memory_space=pltpu.HBM)] * 3,
        out_specs=(pl.BlockSpec(memory_space=pltpu.VMEM), pl.BlockSpec(memory_space=pltpu.VMEM)),
        scratch_shapes=[
            vmem((TOK, HALF), bf16),
            vmem((TOK, HALF), bf16),
            vmem((TOK, WIDTH), bf16),
            vmem((HEADS, WIDTH), bf16),
            vmem((HALF, TOK), bf16),
            vmem((HALF, WIDTH), bf16),
            vmem((HALF, WIDTH), bf16),
            vmem((HALF, WIDTH), bf16),
            vmem((HALF, WIDTH), bf16),
            vmem((2, HALF, max(RAW, 128)), bf16),
            vmem((8, 128), f32),
            vmem((CHIPS, 8, 128), f32),
            vmem((1, 128), f32),
            vmem((GROUP, 1, 128), f32),
            vmem((HALF, HALF), f32),
            vmem((2, 128), f32),
            vmem((GROUP, 2, 128), f32),
            vmem((2, 128), f32),
            vmem((CHIPS, 2, 128), f32),
            vmem((4, CHIPS, 128), f32),
            dma((3,)),
            dma,
            dma,
            dma((CHUNKS,)),
            dma,
            dma,
            dma,
            dma((PIECES,)),
            dma,
            dma,
            dma,
            dma,
            dma,
            dma,
            dma,
            dma,
            dma,
            dma((N_RECV,)),
            dma,
            dma,
        ],
        compiler_params=pltpu.CompilerParams(
            collective_id=0, has_side_effects=True, vmem_limit_bytes=40 << 20
        ),
        cost_estimate=pl.CostEstimate(flops=8 << 30, bytes_accessed=14 << 20, transcendentals=0),
    )(context, upstream, out_proj)
    return pl.pallas_call(
        store,
        out_shape=(OUT_COMB, OUT_CG),
        in_specs=[pl.BlockSpec(memory_space=pl.ANY)] * 2,
        out_specs=[pl.BlockSpec(memory_space=pltpu.HBM)] * 2,
        compiler_params=pltpu.CompilerParams(vmem_limit_bytes=1 << 20),
        scratch_shapes=[pltpu.SemaphoreType.DMA((OUT_PARTS + 1,))],
    )(*results)


OUT_COMB = jax.ShapeDtypeStruct((HEADS, WIDTH), jnp.bfloat16)
OUT_CG = jax.ShapeDtypeStruct((TOK, HEADS), jnp.bfloat16)


def solution(mesh):
    in_specs = (P("dp", "mp"), P("dp", None), P("mp", None))
    out_specs = (P("mp", None), P("dp", "mp"))
    return jax.shard_map(shards, mesh=mesh, in_specs=in_specs, out_specs=out_specs, check_vma=False)
```
